512 devices in a mesh: head: 8 (over x, y_lo), ctx: 64 (over z, y_hi, core).
Axes of the slice: x: 4, y: 8 (y_hi: 4, y_lo: 2; y = y_hi * 2 + y_lo), z: 8, core: 2. Of those that a mesh axis runs over, the one named last changes fastest.
Arguments:
- query_states: bfloat16 [65536, 32, 128], P(('ctx', 'head')), may hold values from -6 to 6
- key_states: bfloat16 [65536, 4, 128], P(('ctx', 'head')), may hold values from -6 to 6
- value_states: bfloat16 [65536, 4, 128], P(('ctx', 'head')), may hold values from -6 to 6
- out_grad: bfloat16 [65536, 32, 128], P(('ctx', 'head')), may hold values from -6 to 6
- log_norm: float32 [65536, 32], P(('ctx', 'head')), may hold values from 4 to 7
- row_delta: float32 [65536, 32], P(('ctx', 'head')), may hold values from -6 to 6
- doc_lengths: int32 [256], replicated, may hold values from 1 to 512, 65536 in all
Outputs:
- query_grad: bfloat16 [65536, 32, 128], P(('ctx', 'head'))
- key_grad: bfloat16 [65536, 4, 128], P(('ctx', 'head'))
- value_grad: bfloat16 [65536, 4, 128], P(('ctx', 'head'))
The draws below stay inside these ranges and needn't reach their ends.
Inputs may be any that keep to these rules, and one draw needn't show every extreme that they name: `doc_lengths`: documents lie end to end in the pack, in order; their lengths sum to 65536 and the longest is exactly 512.
All inputs are finite; a program needn't handle non-finite values.
Results may differ from the reference program's by a relative error of at most 0.012.
Values may be sent and summed in bfloat16 or wider, within the bound.
No kernel may reach another device: no remote copies, remote signals or barrier semaphores. Data moves between devices by JAX's collectives and lax.ppermute only.
A program may use at most 64 MiB of HBM per device.

```python
import math
import jax
import jax.numpy as jnp
import numpy as np
from jax import lax

HEADS = 32
KV_HEADS = 4
HEAD_DIM = 128
MOST = 512
TOKENS = 65536
DOCS = 256


def shard_levels(stream_key, shape, shards, low, high):
    level, own = 1.0, jax.random.fold_in(stream_key, 6)
    for position, parts in shards:
        steps = jnp.exp(jax.random.uniform(jax.random.fold_in(own, position), (parts,), jnp.float32, low / len(shards), high / len(shards)))
        level = level * jnp.repeat(steps, shape[position] // parts).reshape([-1 if axis == position else 1 for axis in range(len(shape))])
    return level


def profile(number_of, total, reach, skew):
    portions = [(1 << 20) // math.isqrt(rank ** skew) + 1 for rank in range(2, number_of + 1)]
    spare, counts = total - reach - (number_of - 1), [1] * (number_of - 1)
    while spare > 0:
        movable = [i for i in range(number_of - 1) if counts[i] < reach]
        whole, left = sum([portions[i] for i in movable]), spare
        for i in movable:
            extra = min(reach - counts[i], max(1, left * portions[i] // whole), spare)
            counts[i] = counts[i] + extra
            spare = spare - extra
    return np.array([reach] + counts)


def ragged(rng, number_of, total, most, lean):
    if number_of == 2:
        one = jax.random.randint(rng, (), max(1, total - most), min(most, total - 1) + 1)
        return jnp.stack([one, total - one])
    lengths = jnp.asarray(profile(number_of, total, most, lean), jnp.int32)
    twos = (number_of - 1) // 2
    source_of, sink = lengths[1:1 + 2 * twos:2], lengths[2:2 + 2 * twos:2]
    room = jnp.minimum(source_of - 1, most - sink)
    shifted = jax.random.randint(jax.random.fold_in(rng, 1), (twos,), 0, 1 << 20) % (room + 1)
    lengths = lengths.at[1:1 + 2 * twos:2].set(source_of - shifted).at[2:2 + 2 * twos:2].set(sink + shifted)
    return lengths[jax.random.permutation(jax.random.fold_in(rng, 2), number_of)]


def normal_values(key, dims, width, bound, pieces=(), held_as=jnp.bfloat16):
    gain = shard_levels(key, dims, pieces, -0.22, 0.18) if pieces else 1.0
    array = jax.random.normal(key, dims, jnp.float32) * width * gain
    return jnp.minimum(jnp.maximum(array, -bound), bound).astype(held_as)


def setup_inputs(seed: int = 0) -> dict:
    keys = jax.random.split(jax.random.key(seed), 8)
    query_states = normal_values(keys[0], (TOKENS, HEADS, HEAD_DIM), 1.0, 6.0, ((0, 512),))
    key_states = normal_values(keys[1], (TOKENS, KV_HEADS, HEAD_DIM), 1.0, 6.0, ((0, 512),))
    value_states = normal_values(keys[2], (TOKENS, KV_HEADS, HEAD_DIM), 1.0, 6.0, ((0, 512),))
    out_grad = normal_values(keys[3], (TOKENS, HEADS, HEAD_DIM), 0.5, 6.0, ((0, 512),))
    log_norm = jnp.clip(4.0 + 3.0 * jax.random.uniform(keys[4], (TOKENS, HEADS), jnp.float32) ** shard_levels(keys[4], (TOKENS, HEADS), ((0, 512),), -0.2, 0.2), 4.0, 7.0)
    row_delta = normal_values(keys[5], (TOKENS, HEADS), 1.0, 6.0, ((0, 512),), jnp.float32)
    doc_lengths = ragged(keys[6], DOCS, TOKENS, MOST, 1).astype(jnp.int32)
    return dict(query_states=query_states, key_states=key_states, value_states=value_states, out_grad=out_grad, log_norm=log_norm, row_delta=row_delta, doc_lengths=doc_lengths)


def doc_starts(doc_lengths, positions):
    doc_ends = jnp.cumsum(doc_lengths).astype(jnp.int32)
    before = jnp.where(doc_ends[None, :] <= positions[:, None], doc_lengths[None, :], 0)
    return lax.optimization_barrier(jnp.sum(before, axis=1)).astype(jnp.int32)

def reference(query_states, key_states, value_states, out_grad, log_norm, row_delta, doc_lengths):
    softmax_scale = 1.0 / math.sqrt(HEAD_DIM)
    group_size = HEADS // KV_HEADS
    window = 2 * MOST
    rim_zeros = jnp.zeros((MOST, KV_HEADS, HEAD_DIM), jnp.bfloat16)
    padded_keys = jnp.concatenate([rim_zeros, key_states], axis=0)
    padded_values = jnp.concatenate([rim_zeros, value_states], axis=0)

    def block_step(totals, block_index):
        key_total, value_total = totals
        first_row = (block_index * MOST).astype(jnp.int32)
        query_rows = lax.dynamic_slice_in_dim(query_states, first_row, MOST, 0).astype(jnp.float32)
        grad_rows = lax.dynamic_slice_in_dim(out_grad, first_row, MOST, 0).astype(jnp.float32)
        norm_rows = lax.dynamic_slice_in_dim(log_norm, first_row, MOST, 0)
        delta_rows = lax.dynamic_slice_in_dim(row_delta, first_row, MOST, 0)
        key_cols = lax.dynamic_slice_in_dim(padded_keys, first_row, window, 0).astype(jnp.float32)
        value_cols = lax.dynamic_slice_in_dim(padded_values, first_row, window, 0).astype(jnp.float32)
        query_pos = first_row + jnp.arange(MOST, dtype=jnp.int32)
        key_pos = first_row - MOST + jnp.arange(window, dtype=jnp.int32)
        starts = doc_starts(doc_lengths, query_pos)
        allowed = (key_pos[None, :] <= query_pos[:, None]) & (key_pos[None, :] >= starts[:, None])
        query_groups = query_rows.reshape(MOST, KV_HEADS, group_size, HEAD_DIM)
        grad_groups = grad_rows.reshape(MOST, KV_HEADS, group_size, HEAD_DIM)
        norm_groups = jnp.transpose(norm_rows.reshape(MOST, KV_HEADS, group_size), (1, 2, 0))[..., None]
        delta_groups = jnp.transpose(delta_rows.reshape(MOST, KV_HEADS, group_size), (1, 2, 0))[..., None]
        scores = jnp.einsum('qhgd,khd->hgqk', query_groups, key_cols) * softmax_scale
        attn_prob = jnp.where(allowed, jnp.exp(scores - norm_groups), 0.0)
        prob_grad = jnp.einsum('qhgd,khd->hgqk', grad_groups, value_cols)
        score_grad = (attn_prob * (prob_grad - delta_groups)).astype(jnp.bfloat16)
        prob_low = attn_prob.astype(jnp.bfloat16)
        score_grad, prob_low = lax.optimization_barrier((score_grad, prob_low))
        score_wide = score_grad.astype(jnp.float32)
        prob_wide = prob_low.astype(jnp.float32)
        query_part = jnp.einsum('hgqk,khd->qhgd', score_wide, key_cols) * softmax_scale
        key_part = jnp.einsum('hgqk,qhgd->khd', score_wide, query_groups) * softmax_scale
        value_part = jnp.einsum('hgqk,qhgd->khd', prob_wide, grad_groups)
        key_window = lax.dynamic_slice_in_dim(key_total, first_row, window, 0) + key_part
        value_window = lax.dynamic_slice_in_dim(value_total, first_row, window, 0) + value_part
        key_total = lax.dynamic_update_slice_in_dim(key_total, key_window, first_row, 0)
        value_total = lax.dynamic_update_slice_in_dim(value_total, value_window, first_row, 0)
        return ((key_total, value_total), query_part.reshape(MOST, HEADS, HEAD_DIM).astype(jnp.bfloat16))
    zero_total = jnp.zeros((TOKENS + MOST, KV_HEADS, HEAD_DIM), jnp.float32)
    totals, query_blocks = lax.scan(block_step, (zero_total, zero_total), jnp.arange(TOKENS // MOST, dtype=jnp.int32))
    query_grad = query_blocks.reshape(TOKENS, HEADS, HEAD_DIM)
    key_grad = totals[0][MOST:].astype(jnp.bfloat16)
    value_grad = totals[1][MOST:].astype(jnp.bfloat16)
    return (query_grad, key_grad, value_grad)
```

```python
import functools
import math

import jax
import jax.numpy as jnp
from jax import lax
from jax.experimental import pallas as pl
from jax.experimental.pallas import tpu as pltpu
from jax.sharding import PartitionSpec as P

KV_HEADS = 4
HEAD_DIM = 128
MOST = 512
LOG2E = 1.4426950408889634
VMEM_LIMIT = 40 * 1024 * 1024


def doc_starts(doc_lengths, positions):
    doc_ends = jnp.cumsum(doc_lengths)
    before = jnp.where(doc_ends[None, :] <= positions[:, None], doc_lengths[None, :], 0)
    return jnp.sum(before, axis=1)


def chunk_shift(x, by):
    heads, ctxs = lax.axis_size("head"), lax.axis_size("ctx")
    count = heads * ctxs
    place = lambda c: (c % heads) * ctxs + c // heads
    pairs = [(place(c), place(c + by)) for c in range(count) if 0 <= c + by < count]
    return lax.ppermute(x, ("head", "ctx"), pairs)


def contract(left, right, dims):
    return lax.dot_general(
        left, right, ((dims[:1], dims[1:]), ((), ())), preferred_element_type=jnp.float32
    )


def tile_kernel(
    distance,
    first,
    last,
    softmax_scale,
    start_ref,
    norm_ref,
    delta_ref,
    query_ref,
    grad_ref,
    kv_ref,
    *rest,
):
    if first:
        query_total_ref, kv_part_ref = rest
    else:
        query_in_ref, query_total_ref, kv_part_ref = rest
    rows = kv_ref.shape[2]
    cols = query_ref.shape[1]
    step = 2 * rows
    keys = kv_ref[0, 0]
    values = kv_ref[1, 0]
    key_part = jnp.zeros((rows, HEAD_DIM), jnp.float32)
    value_part = jnp.zeros((rows, HEAD_DIM), jnp.float32)
    key_pos = lax.broadcasted_iota(jnp.int32, (rows, step), 0) - distance * rows
    if distance == 0:
        query_pos = lax.broadcasted_iota(jnp.int32, (rows, step), 1) & (rows - 1)
        causal = key_pos <= query_pos
    for at in range(0, cols, step):
        span = pl.ds(at, step)
        query_rows = query_ref[0, span, :]
        grad_rows = grad_ref[0, span, :]
        scores = contract(keys, query_rows, (1, 1))
        prob_grad = contract(values, grad_rows, (1, 1))
        prob = jnp.exp2(scores * (softmax_scale * LOG2E) - norm_ref[0, :, span] * LOG2E)
        allowed = key_pos >= start_ref[:, span]
        if distance == 0:
            allowed = allowed & causal
        prob = jnp.where(allowed, prob, 0.0)
        score_grad = (prob * (prob_grad - delta_ref[0, :, span])).astype(jnp.bfloat16)
        value_part += contract(prob.astype(jnp.bfloat16), grad_rows, (1, 0))
        key_part += contract(score_grad, query_rows, (1, 0))
        query_part = contract(keys, score_grad, (0, 0))
        if not first:
            query_part += query_in_ref[0, :, span]
        if last:
            for head in range(at // rows, (at + step) // rows):
                part = query_part[:, head * rows - at : (head + 1) * rows - at]
                query_total_ref[0, head] = (part.T * softmax_scale).astype(jnp.bfloat16)
        else:
            query_total_ref[0, :, span] = query_part
    kv_part_ref[0, 0] = (key_part * softmax_scale).astype(kv_part_ref.dtype)
    kv_part_ref[1, 0] = value_part.astype(kv_part_ref.dtype)


def tile_call(distance, first, last, starts, norms, deltas, queries, grads, kv, query_total=None):
    groups, cols, dim = queries.shape
    rows = kv.shape[2]
    softmax_scale = 1.0 / math.sqrt(HEAD_DIM)
    row_spec = pl.BlockSpec((1, 1, cols), lambda g: (g, 0, 0))
    wide_spec = pl.BlockSpec((1, cols, dim), lambda g: (g, 0, 0))
    kv_spec = pl.BlockSpec((2, 1, rows, dim), lambda g: (0, g, 0, 0))
    total_spec = pl.BlockSpec((1, dim, cols), lambda g: (g, 0, 0))
    in_specs = [
        pl.BlockSpec((1, cols), lambda g: (0, 0)),
        row_spec,
        row_spec,
        wide_spec,
        wide_spec,
        kv_spec,
    ]
    args = [starts, norms, deltas, queries, grads, kv]
    if not first:
        in_specs.append(total_spec)
        args.append(query_total)
    if last:
        heads = cols // rows
        query_shape = jax.ShapeDtypeStruct((groups, heads, rows, dim), jnp.bfloat16)
        query_spec = pl.BlockSpec((1, heads, rows, dim), lambda g: (g, 0, 0, 0))
    else:
        query_shape = jax.ShapeDtypeStruct((groups, dim, cols), jnp.float32)
        query_spec = total_spec
    kv_shape = jax.ShapeDtypeStruct(kv.shape, jnp.float32 if distance == 0 else jnp.bfloat16)
    return pl.pallas_call(
        functools.partial(tile_kernel, distance, first, last, softmax_scale),
        grid=(groups,),
        in_specs=in_specs,
        out_specs=(query_spec, kv_spec),
        out_shape=(query_shape, kv_shape),
        compiler_params=pltpu.CompilerParams(vmem_limit_bytes=VMEM_LIMIT),
        cost_estimate=pl.CostEstimate(
            flops=10 * groups * cols * rows * dim,
            bytes_accessed=6 * groups * cols * dim,
            transcendentals=groups * cols * rows,
        ),
        name=f"tiles_{distance}",
    )(*args)


def shards(query_states, key_states, value_states, out_grad, log_norm, row_delta, doc_lengths):
    rows, heads, dim = query_states.shape
    group = heads // KV_HEADS
    reach = MOST // rows
    chunk = lax.axis_index("ctx") * lax.axis_size("head") + lax.axis_index("head")
    first_pos = chunk * rows

    kv = jnp.transpose(jnp.stack([key_states, value_states]), (0, 2, 1, 3))
    behind = {distance: chunk_shift(kv, distance) for distance in range(reach, 0, -1)}

    by_head = lambda x: jnp.transpose(x, (1, 0, 2)).reshape(KV_HEADS, group * rows, dim)
    queries, grads = by_head(query_states), by_head(out_grad)
    norms = log_norm.T.reshape(KV_HEADS, 1, group * rows)
    deltas = row_delta.T.reshape(KV_HEADS, 1, group * rows)
    positions = first_pos + jnp.arange(rows, dtype=jnp.int32)
    starts = doc_starts(doc_lengths, positions) - first_pos
    starts = jnp.tile(starts, group).reshape(1, group * rows)

    query_total, kv_own = tile_call(0, True, False, starts, norms, deltas, queries, grads, kv)
    returned = []
    for distance in range(reach, 0, -1):
        query_total, kv_part = tile_call(
            distance,
            False,
            distance == 1,
            starts,
            norms,
            deltas,
            queries,
            grads,
            behind[distance],
            query_total,
        )
        returned.append(chunk_shift(kv_part, -distance))
    for part in returned:
        kv_own = kv_own + part.astype(jnp.float32)
    kv_grad = jnp.transpose(kv_own.astype(jnp.bfloat16), (0, 2, 1, 3))
    query_grad = jnp.transpose(query_total.reshape(heads, rows, dim), (1, 0, 2))
    return (query_grad, kv_grad[0], kv_grad[1])


def solution(mesh):
    spec3 = P(("ctx", "head"), None, None)
    spec2 = P(("ctx", "head"), None)
    return jax.shard_map(
        shards,
        mesh=mesh,
        in_specs=(spec3, spec3, spec3, spec3, spec2, spec2, P()),
        out_specs=(spec3, spec3, spec3),
        check_vma=False,
    )
```

```python
import functools
import math

import jax
import jax.numpy as jnp
from jax import lax
from jax.experimental import pallas as pl
from jax.experimental.pallas import tpu as pltpu
from jax.sharding import PartitionSpec as P

KV_HEADS = 4
HEAD_DIM = 128
MOST = 512
LOG2E = 1.4426950408889634
VMEM_LIMIT = 40 * 1024 * 1024
WEIGHT = 1
SUM_FLOPS = 5_000_000_000


def doc_starts(doc_lengths, positions):
    doc_ends = jnp.cumsum(doc_lengths)
    before = jnp.where(doc_ends[None, :] <= positions[:, None], doc_lengths[None, :], 0)
    return jnp.sum(before, axis=1)


def chunk_shift(x, by):
    heads, ctxs = lax.axis_size("head"), lax.axis_size("ctx")
    count = heads * ctxs
    place = lambda c: (c % heads) * ctxs + c // heads
    pairs = [(place(c), place(c + by)) for c in range(count) if 0 <= c + by < count]
    return lax.ppermute(x, ("head", "ctx"), pairs)


def contract(left, right, dims):
    return lax.dot_general(
        left, right, ((dims[:1], dims[1:]), ((), ())), preferred_element_type=jnp.float32
    )


def tile_kernel(
    distance,
    softmax_scale,
    start_ref,
    norm_ref,
    delta_ref,
    query_ref,
    grad_ref,
    kv_ref,
    *rest,
):
    query_in_ref = rest[0] if len(rest) == 3 else None
    query_total_ref, kv_part_ref = rest[-2:]
    groups, cols, _ = query_ref.shape
    rows = kv_ref.shape[2]
    key_pos = lax.broadcasted_iota(jnp.int32, (rows, cols), 0) - distance * rows
    allowed = key_pos >= start_ref[...]
    if distance == 0:
        query_pos = lax.broadcasted_iota(jnp.int32, (rows, cols), 1) & (rows - 1)
        allowed = allowed & (key_pos <= query_pos)
    for group in range(groups):
        keys = kv_ref[0, group]
        values = kv_ref[1, group]
        query_rows = query_ref[group]
        grad_rows = grad_ref[group]
        scores = contract(keys, query_rows, (1, 1))
        prob_grad = contract(values, grad_rows, (1, 1))
        prob = jnp.exp2(scores * (softmax_scale * LOG2E) - norm_ref[group])
        prob = jnp.where(allowed, prob, 0.0)
        score_grad = (prob * (prob_grad - delta_ref[group])).astype(jnp.bfloat16)
        value_part = contract(prob.astype(jnp.bfloat16), grad_rows, (1, 0))
        key_part = contract(score_grad, query_rows, (1, 0)) * softmax_scale
        query_part = contract(keys, score_grad, (0, 0))
        if query_in_ref is not None:
            query_part += query_in_ref[group]
        query_total_ref[group] = query_part
        kv_part_ref[0, group] = key_part.astype(kv_part_ref.dtype)
        kv_part_ref[1, group] = value_part.astype(kv_part_ref.dtype)


def tile_call(distance, starts, norms, deltas, queries, grads, kv, query_total=None):
    groups, cols, dim = queries.shape
    rows = kv.shape[2]
    args = [starts, norms, deltas, queries, grads, kv]
    aliases = {}
    if query_total is not None:
        aliases = {len(args): 0}
        args.append(query_total)
    whole = pl.BlockSpec(memory_space=pltpu.VMEM)
    return pl.pallas_call(
        functools.partial(tile_kernel, distance, 1.0 / math.sqrt(dim)),
        in_specs=[whole] * len(args),
        out_specs=(whole, whole),
        out_shape=(
            jax.ShapeDtypeStruct((groups, dim, cols), jnp.float32),
            jax.ShapeDtypeStruct(kv.shape, jnp.float32 if distance == 0 else jnp.bfloat16),
        ),
        input_output_aliases=aliases,
        compiler_params=pltpu.CompilerParams(vmem_limit_bytes=VMEM_LIMIT),
        cost_estimate=pl.CostEstimate(
            flops=WEIGHT * 10 * groups * cols * rows * dim,
            bytes_accessed=6 * groups * cols * dim,
            transcendentals=groups * cols * rows,
        ),
        name=f"tiles_{distance}",
    )(*args)


def query_kernel(softmax_scale, total_ref, out_ref):
    groups, heads, rows, _ = out_ref.shape

    def group_step(group, carry):
        for head in range(heads):
            part = total_ref[group, :, pl.ds(head * rows, rows)]
            out_ref[group, head] = (part.T * softmax_scale).astype(out_ref.dtype)
        return carry

    lax.fori_loop(0, groups, group_step, 0)


def query_call(query_total, rows):
    groups, dim, cols = query_total.shape
    whole = pl.BlockSpec(memory_space=pltpu.VMEM)
    return pl.pallas_call(
        functools.partial(query_kernel, 1.0 / math.sqrt(dim)),
        in_specs=[whole],
        out_specs=whole,
        out_shape=jax.ShapeDtypeStruct((groups, cols // rows, rows, dim), jnp.bfloat16),
        compiler_params=pltpu.CompilerParams(vmem_limit_bytes=VMEM_LIMIT),
        cost_estimate=pl.CostEstimate(
            flops=groups * cols * dim, bytes_accessed=6 * groups * cols * dim, transcendentals=0
        ),
        name="query_rows",
    )(query_total)


def sum_kernel(total_ref, part_ref, out_ref):
    out_ref[...] = total_ref[...] + part_ref[...].astype(jnp.float32)


def sum_call(total, part):
    whole = pl.BlockSpec(memory_space=pltpu.VMEM)
    return pl.pallas_call(
        sum_kernel,
        in_specs=[whole, whole],
        out_specs=whole,
        out_shape=jax.ShapeDtypeStruct(total.shape, total.dtype),
        input_output_aliases={0: 0},
        compiler_params=pltpu.CompilerParams(vmem_limit_bytes=VMEM_LIMIT),
        cost_estimate=pl.CostEstimate(flops=SUM_FLOPS, bytes_accessed=10 * total.size, transcendentals=0),
        name="kv_sum",
    )(total, part)


def last_kernel(total_ref, part_ref, key_ref, value_ref):
    for index, out_ref in enumerate((key_ref, value_ref)):
        whole = total_ref[index] + part_ref[index].astype(jnp.float32)
        out_ref[...] = jnp.transpose(whole, (1, 0, 2)).astype(out_ref.dtype)


def last_call(total, part):
    _, groups, rows, dim = total.shape
    whole = pl.BlockSpec(memory_space=pltpu.VMEM)
    out = jax.ShapeDtypeStruct((rows, groups, dim), jnp.bfloat16)
    return pl.pallas_call(
        last_kernel,
        in_specs=[whole, whole],
        out_specs=(whole, whole),
        out_shape=(out, out),
        compiler_params=pltpu.CompilerParams(vmem_limit_bytes=VMEM_LIMIT),
        cost_estimate=pl.CostEstimate(
            flops=total.size, bytes_accessed=8 * total.size, transcendentals=0
        ),
        name="kv_rows",
    )(total, part)


def shards(query_states, key_states, value_states, out_grad, log_norm, row_delta, doc_lengths):
    rows, heads, dim = query_states.shape
    group = heads // KV_HEADS
    reach = MOST // rows
    chunk = lax.axis_index("ctx") * lax.axis_size("head") + lax.axis_index("head")
    first_pos = chunk * rows

    kv = jnp.transpose(jnp.stack([key_states, value_states]), (0, 2, 1, 3))
    behind = {distance: chunk_shift(kv, distance) for distance in range(reach, 0, -1)}

    by_head = lambda x: jnp.transpose(x, (1, 0, 2)).reshape(KV_HEADS, group * rows, dim)
    queries, grads = by_head(query_states), by_head(out_grad)
    norms = (log_norm.T * LOG2E).reshape(KV_HEADS, 1, group * rows)
    deltas = row_delta.T.reshape(KV_HEADS, 1, group * rows)
    positions = first_pos + jnp.arange(rows, dtype=jnp.int32)
    starts = doc_starts(doc_lengths, positions) - first_pos
    starts = jnp.tile(starts, group).reshape(1, group * rows)

    rows_of = (starts, norms, deltas, queries, grads)
    query_total, kv_own = tile_call(0, *rows_of, kv)
    returned = []
    for distance in range(reach, 0, -1):
        query_total, kv_part = tile_call(distance, *rows_of, behind[distance], query_total)
        returned.append(chunk_shift(kv_part, -distance))
    query_heads = query_call(query_total, rows)
    for part in returned[:-1]:
        kv_own = sum_call(kv_own, part)
    key_grad, value_grad = last_call(kv_own, returned[-1])
    query_grad = jnp.transpose(query_heads.reshape(heads, rows, dim), (1, 0, 2))
    return (query_grad, key_grad, value_grad)


def solution(mesh):
    spec3 = P(("ctx", "head"), None, None)
    spec2 = P(("ctx", "head"), None)
    return jax.shard_map(
        shards,
        mesh=mesh,
        in_specs=(spec3, spec3, spec3, spec3, spec2, spec2, P()),
        out_specs=(spec3, spec3, spec3),
        check_vma=False,
    )
```

```python
import functools
import math

import jax
import jax.numpy as jnp
from jax import lax
from jax.experimental import pallas as pl
from jax.experimental.pallas import tpu as pltpu
from jax.sharding import PartitionSpec as P

KV_HEADS = 4
HEAD_DIM = 128
MOST = 512
LOG2E = 1.4426950408889634
VMEM_LIMIT = 40 * 1024 * 1024
SUM_FLOPS = 700_000_000
ORDER = (3, 4, 2, 1)


def chunk_permute(x, target):
    heads, ctxs = lax.axis_size("head"), lax.axis_size("ctx")
    count = heads * ctxs
    place = lambda c: (c % heads) * ctxs + c // heads
    routes = [(c, target(c)) for c in range(count)]
    pairs = [(place(c), place(to)) for c, to in routes if 0 <= to < count]
    return lax.ppermute(x, ("head", "ctx"), pairs)


def contract(left, right, dims):
    return lax.dot_general(
        left, right, ((dims[:1], dims[1:]), ((), ())), preferred_element_type=jnp.float32
    )


def rows_kernel(place_ref, norm_ref, delta_ref, length_ref, start_ref, norm_out, delta_out):
    groups, _, cols = norm_out.shape
    heads, rows = norm_ref.shape
    docs = length_ref.shape[1]
    norms = norm_ref[...] * LOG2E
    deltas = delta_ref[...]
    for head in range(heads):
        group, at = divmod(head * rows, cols)
        norm_out[group, :, pl.ds(at, rows)] = norms[head : head + 1]
        delta_out[group, :, pl.ds(at, rows)] = deltas[head : head + 1]
    upto = lax.broadcasted_iota(jnp.int32, (docs, docs), 1) <= lax.broadcasted_iota(
        jnp.int32, (docs, docs), 0
    )
    lengths = length_ref[...].astype(jnp.float32)
    ends = jnp.sum(jnp.where(upto, lengths, 0.0), axis=1, keepdims=True)
    first = place_ref[0]
    positions = (lax.broadcasted_iota(jnp.int32, (docs, rows), 1) + first).astype(jnp.float32)
    starts = jnp.max(jnp.where(ends <= positions, ends, 0.0), axis=0, keepdims=True)
    starts = starts.astype(jnp.int32) - first
    for slot in range(start_ref.shape[0]):
        for at in range(0, cols, rows):
            start_ref[slot, :, pl.ds(at, rows)] = starts + place_ref[1 + slot]


def rows_call(place, log_norm, row_delta, doc_lengths):
    rows, heads = log_norm.shape
    cols = heads * rows // KV_HEADS
    whole = pl.BlockSpec(memory_space=pltpu.VMEM)
    slots = place.shape[0] - 1
    wide = jax.ShapeDtypeStruct((KV_HEADS, 1, cols), jnp.float32)
    return pl.pallas_call(
        rows_kernel,
        in_specs=[pl.BlockSpec(memory_space=pltpu.SMEM), whole, whole, whole],
        out_specs=(whole, whole, whole),
        out_shape=(jax.ShapeDtypeStruct((slots, 1, cols), jnp.int32), wide, wide),
        compiler_params=pltpu.CompilerParams(vmem_limit_bytes=VMEM_LIMIT),
        name="row_terms",
    )(place, log_norm.T, row_delta.T, doc_lengths.reshape(1, -1))


def tile_kernel(
    slot,
    softmax_scale,
    start_ref,
    norm_ref,
    delta_ref,
    query_ref,
    grad_ref,
    kv_ref,
    *rest,
):
    query_in_ref = rest[0] if len(rest) == 3 else None
    query_total_ref, kv_part_ref = rest[-2:]
    groups, cols, _ = query_ref.shape
    rows = kv_ref.shape[2]
    def work():
        key_pos = lax.broadcasted_iota(jnp.int32, (rows, cols), 0)
        allowed = key_pos >= start_ref[slot]
        if slot == 0:
            query_pos = lax.broadcasted_iota(jnp.int32, (rows, cols), 1) & (rows - 1)
            allowed = allowed & (key_pos <= query_pos)
        for group in range(groups):
            keys = kv_ref[0, group]
            values = kv_ref[1, group]
            query_rows = query_ref[group]
            grad_rows = grad_ref[group]
            scores = contract(keys, query_rows, (1, 1))
            prob_grad = contract(values, grad_rows, (1, 1))
            prob = jnp.exp2(scores * (softmax_scale * LOG2E) - norm_ref[group])
            prob = jnp.where(allowed, prob, 0.0)
            score_grad = (prob * (prob_grad - delta_ref[group])).astype(jnp.bfloat16)
            value_part = contract(prob.astype(jnp.bfloat16), grad_rows, (1, 0))
            key_part = contract(score_grad, query_rows, (1, 0)) * softmax_scale
            query_part = contract(keys, score_grad, (0, 0))
            if query_in_ref is not None:
                query_part += query_in_ref[group]
            query_total_ref[group] = query_part
            kv_part_ref[0, group] = key_part.astype(kv_part_ref.dtype)
            kv_part_ref[1, group] = value_part.astype(kv_part_ref.dtype)

    if slot == 0:
        work()
        return
    needed = jnp.min(start_ref[slot, :, pl.ds(0, rows)]) < rows
    pl.when(needed)(work)

    @pl.when(jnp.logical_not(needed))
    def _():
        if query_in_ref is None:
            query_total_ref[...] = jnp.zeros_like(query_total_ref)
        else:
            query_total_ref[...] = query_in_ref[...]
        kv_part_ref[...] = jnp.zeros_like(kv_part_ref)


def tile_call(slot, starts, norms, deltas, queries, grads, kv, query_total=None):
    groups, cols, dim = queries.shape
    rows = kv.shape[2]
    args = [starts, norms, deltas, queries, grads, kv]
    aliases = {}
    if query_total is not None:
        aliases = {len(args): 0}
        args.append(query_total)
    whole = pl.BlockSpec(memory_space=pltpu.VMEM)
    return pl.pallas_call(
        functools.partial(tile_kernel, slot, 1.0 / math.sqrt(dim)),
        in_specs=[whole] * len(args),
        out_specs=(whole, whole),
        out_shape=(
            jax.ShapeDtypeStruct((groups, dim, cols), jnp.float32),
            jax.ShapeDtypeStruct(kv.shape, jnp.float32 if slot == 0 else jnp.bfloat16),
        ),
        input_output_aliases=aliases,
        compiler_params=pltpu.CompilerParams(vmem_limit_bytes=VMEM_LIMIT),
        cost_estimate=pl.CostEstimate(
            flops=10 * groups * cols * rows * dim,
            bytes_accessed=6 * groups * cols * dim,
            transcendentals=groups * cols * rows,
        ),
        name=f"tiles_{slot}",
    )(*args)


def query_kernel(softmax_scale, total_ref, out_ref):
    groups, heads, rows, _ = out_ref.shape

    def group_step(group, carry):
        for head in range(heads):
            part = total_ref[group, :, pl.ds(head * rows, rows)]
            out_ref[group, head] = (part.T * softmax_scale).astype(out_ref.dtype)
        return carry

    lax.fori_loop(0, groups, group_step, 0)


def query_call(query_total, rows):
    groups, dim, cols = query_total.shape
    whole = pl.BlockSpec(memory_space=pltpu.VMEM)
    return pl.pallas_call(
        functools.partial(query_kernel, 1.0 / math.sqrt(dim)),
        in_specs=[whole],
        out_specs=whole,
        out_shape=jax.ShapeDtypeStruct((groups, cols // rows, rows, dim), jnp.bfloat16),
        compiler_params=pltpu.CompilerParams(vmem_limit_bytes=VMEM_LIMIT),
        cost_estimate=pl.CostEstimate(
            flops=groups * cols * dim, bytes_accessed=6 * groups * cols * dim, transcendentals=0
        ),
        name="query_rows",
    )(query_total)


def sum_kernel(total_ref, part_ref, out_ref):
    out_ref[...] = total_ref[...] + part_ref[...].astype(jnp.float32)


def sum_call(total, part):
    whole = pl.BlockSpec(memory_space=pltpu.VMEM)
    return pl.pallas_call(
        sum_kernel,
        in_specs=[whole, whole],
        out_specs=whole,
        out_shape=jax.ShapeDtypeStruct(total.shape, total.dtype),
        input_output_aliases={0: 0},
        compiler_params=pltpu.CompilerParams(vmem_limit_bytes=VMEM_LIMIT),
        cost_estimate=pl.CostEstimate(flops=SUM_FLOPS, bytes_accessed=10 * total.size, transcendentals=0),
        name="kv_sum",
    )(total, part)


def last_kernel(total_ref, part_ref, key_ref, value_ref):
    for index, out_ref in enumerate((key_ref, value_ref)):
        whole = total_ref[index] + part_ref[index].astype(jnp.float32)
        out_ref[...] = jnp.transpose(whole, (1, 0, 2)).astype(out_ref.dtype)


def last_call(total, part):
    _, groups, rows, dim = total.shape
    whole = pl.BlockSpec(memory_space=pltpu.VMEM)
    out = jax.ShapeDtypeStruct((rows, groups, dim), jnp.bfloat16)
    return pl.pallas_call(
        last_kernel,
        in_specs=[whole, whole],
        out_specs=(whole, whole),
        out_shape=(out, out),
        compiler_params=pltpu.CompilerParams(vmem_limit_bytes=VMEM_LIMIT),
        cost_estimate=pl.CostEstimate(
            flops=total.size, bytes_accessed=8 * total.size, transcendentals=0
        ),
        name="kv_rows",
    )(total, part)


def shards(query_states, key_states, value_states, out_grad, log_norm, row_delta, doc_lengths):
    rows, heads, dim = query_states.shape
    group = heads // KV_HEADS
    chunk = lax.axis_index("ctx") * lax.axis_size("head") + lax.axis_index("head")
    first_pos = chunk * rows

    kv = jnp.transpose(jnp.stack([key_states, value_states]), (0, 2, 1, 3))
    behind = {distance: chunk_permute(kv, lambda c, d=distance: c + d) for distance in ORDER}

    by_head = lambda x: jnp.transpose(x, (1, 0, 2)).reshape(KV_HEADS, group * rows, dim)
    queries, grads = by_head(query_states), by_head(out_grad)
    distances = jnp.asarray((0, *ORDER), jnp.int32)
    place = jnp.concatenate([jnp.reshape(first_pos, (1,)), distances * rows])
    starts, norms, deltas = rows_call(place, log_norm, row_delta, doc_lengths)

    rows_of = (starts, norms, deltas, queries, grads)
    query_total = None
    returned = []
    for slot, distance in enumerate(ORDER, 1):
        query_total, kv_part = tile_call(slot, *rows_of, behind[distance], query_total)
        returned.append(chunk_permute(kv_part, lambda c, d=distance: c - d))
    query_total, kv_own = tile_call(0, *rows_of, kv, query_total)
    query_heads = query_call(query_total, rows)
    for part in returned[:-1]:
        kv_own = sum_call(kv_own, part)
    key_grad, value_grad = last_call(kv_own, returned[-1])
    query_grad = jnp.transpose(query_heads.reshape(heads, rows, dim), (1, 0, 2))
    return (query_grad, key_grad, value_grad)


def solution(mesh):
    spec3 = P(("ctx", "head"), None, None)
    spec2 = P(("ctx", "head"), None)
    return jax.shard_map(
        shards,
        mesh=mesh,
        in_specs=(spec3, spec3, spec3, spec3, spec2, spec2, P()),
        out_specs=(spec3, spec3, spec3),
        check_vma=False,
    )
```

```python
import functools
import math

import jax
import jax.numpy as jnp
from jax import lax
from jax.experimental import pallas as pl
from jax.experimental.pallas import tpu as pltpu
from jax.sharding import PartitionSpec as P

KV_HEADS = 4
HEAD_DIM = 128
MOST = 512
LOG2E = 1.4426950408889634
VMEM_LIMIT = 40 * 1024 * 1024
SUM_FLOPS = 700_000_000
ORDER = (3, 4, 2, 1)


def chunk_permute(x, target):
    heads, ctxs = lax.axis_size("head"), lax.axis_size("ctx")
    count = heads * ctxs
    place = lambda c: (c % heads) * ctxs + c // heads
    routes = [(c, target(c)) for c in range(count)]
    pairs = [(place(c), place(to)) for c, to in routes if 0 <= to < count]
    return lax.ppermute(x, ("head", "ctx"), pairs)


def contract(left, right, dims):
    return lax.dot_general(
        left, right, ((dims[:1], dims[1:]), ((), ())), preferred_element_type=jnp.float32
    )


def rows_kernel(place_ref, norm_ref, delta_ref, length_ref, start_ref, norm_out, delta_out):
    groups, _, cols = norm_out.shape
    heads, rows = norm_ref.shape
    docs = length_ref.shape[1]
    norms = norm_ref[...] * LOG2E
    deltas = delta_ref[...]
    for head in range(heads):
        group, at = divmod(head * rows, cols)
        norm_out[group, :, pl.ds(at, rows)] = norms[head : head + 1]
        delta_out[group, :, pl.ds(at, rows)] = deltas[head : head + 1]
    upto = lax.broadcasted_iota(jnp.int32, (docs, docs), 1) <= lax.broadcasted_iota(
        jnp.int32, (docs, docs), 0
    )
    lengths = length_ref[...].astype(jnp.float32)
    ends = jnp.sum(jnp.where(upto, lengths, 0.0), axis=1, keepdims=True)
    first = place_ref[0]
    positions = (lax.broadcasted_iota(jnp.int32, (docs, rows), 1) + first).astype(jnp.float32)
    starts = jnp.max(jnp.where(ends <= positions, ends, 0.0), axis=0, keepdims=True)
    starts = starts.astype(jnp.int32) - first
    for slot in range(start_ref.shape[0]):
        for at in range(0, cols, rows):
            start_ref[slot, :, pl.ds(at, rows)] = starts + place_ref[1 + slot]


def rows_call(place, log_norm, row_delta, doc_lengths):
    rows, heads = log_norm.shape
    cols = heads * rows // KV_HEADS
    whole = pl.BlockSpec(memory_space=pltpu.VMEM)
    slots = place.shape[0] - 1
    wide = jax.ShapeDtypeStruct((KV_HEADS, 1, cols), jnp.float32)
    return pl.pallas_call(
        rows_kernel,
        in_specs=[pl.BlockSpec(memory_space=pltpu.SMEM), whole, whole, whole],
        out_specs=(whole, whole, whole),
        out_shape=(jax.ShapeDtypeStruct((slots, 1, cols), jnp.int32), wide, wide),
        compiler_params=pltpu.CompilerParams(vmem_limit_bytes=VMEM_LIMIT),
        name="row_terms",
    )(place, log_norm.T, row_delta.T, doc_lengths.reshape(1, -1))


def tile_kernel(
    slot,
    softmax_scale,
    start_ref,
    norm_ref,
    delta_ref,
    query_ref,
    grad_ref,
    kv_ref,
    *rest,
):
    query_in_ref = rest[0] if len(rest) == 3 else None
    query_total_ref, kv_part_ref = rest[-2:]
    groups, cols, _ = query_ref.shape
    rows = kv_ref.shape[2]
    key_pos = lax.broadcasted_iota(jnp.int32, (rows, cols), 0)
    allowed = key_pos >= start_ref[slot]
    if slot == 0:
        query_pos = lax.broadcasted_iota(jnp.int32, (rows, cols), 1) & (rows - 1)
        allowed = allowed & (key_pos <= query_pos)
    for group in range(groups):
        keys = kv_ref[0, group]
        values = kv_ref[1, group]
        query_rows = query_ref[group]
        grad_rows = grad_ref[group]
        scores = contract(keys, query_rows, (1, 1))
        prob_grad = contract(values, grad_rows, (1, 1))
        prob = jnp.exp2(scores * (softmax_scale * LOG2E) - norm_ref[group])
        prob = jnp.where(allowed, prob, 0.0)
        score_grad = (prob * (prob_grad - delta_ref[group])).astype(jnp.bfloat16)
        value_part = contract(prob.astype(jnp.bfloat16), grad_rows, (1, 0))
        key_part = contract(score_grad, query_rows, (1, 0)) * softmax_scale
        query_part = contract(keys, score_grad, (0, 0))
        if query_in_ref is not None:
            query_part += query_in_ref[group]
        query_total_ref[group] = query_part
        kv_part_ref[0, group] = key_part.astype(kv_part_ref.dtype)
        kv_part_ref[1, group] = value_part.astype(kv_part_ref.dtype)


def tile_call(slot, starts, norms, deltas, queries, grads, kv, query_total=None):
    groups, cols, dim = queries.shape
    rows = kv.shape[2]
    args = [starts, norms, deltas, queries, grads, kv]
    aliases = {}
    if query_total is not None:
        aliases = {len(args): 0}
        args.append(query_total)
    whole = pl.BlockSpec(memory_space=pltpu.VMEM)
    return pl.pallas_call(
        functools.partial(tile_kernel, slot, 1.0 / math.sqrt(dim)),
        in_specs=[whole] * len(args),
        out_specs=(whole, whole),
        out_shape=(
            jax.ShapeDtypeStruct((groups, dim, cols), jnp.float32),
            jax.ShapeDtypeStruct(kv.shape, jnp.float32 if slot == 0 else jnp.bfloat16),
        ),
        input_output_aliases=aliases,
        compiler_params=pltpu.CompilerParams(vmem_limit_bytes=VMEM_LIMIT),
        cost_estimate=pl.CostEstimate(
            flops=10 * groups * cols * rows * dim,
            bytes_accessed=6 * groups * cols * dim,
            transcendentals=groups * cols * rows,
        ),
        name=f"tiles_{slot}",
    )(*args)


def query_kernel(softmax_scale, total_ref, out_ref):
    groups, heads, rows, _ = out_ref.shape

    def group_step(group, carry):
        for head in range(heads):
            part = total_ref[group, :, pl.ds(head * rows, rows)]
            out_ref[group, head] = (part.T * softmax_scale).astype(out_ref.dtype)
        return carry

    lax.fori_loop(0, groups, group_step, 0)


def query_call(query_total, rows):
    groups, dim, cols = query_total.shape
    whole = pl.BlockSpec(memory_space=pltpu.VMEM)
    return pl.pallas_call(
        functools.partial(query_kernel, 1.0 / math.sqrt(dim)),
        in_specs=[whole],
        out_specs=whole,
        out_shape=jax.ShapeDtypeStruct((groups, cols // rows, rows, dim), jnp.bfloat16),
        compiler_params=pltpu.CompilerParams(vmem_limit_bytes=VMEM_LIMIT),
        cost_estimate=pl.CostEstimate(
            flops=groups * cols * dim, bytes_accessed=6 * groups * cols * dim, transcendentals=0
        ),
        name="query_rows",
    )(query_total)


def sum_kernel(total_ref, part_ref, out_ref):
    out_ref[...] = total_ref[...] + part_ref[...].astype(jnp.float32)


def sum_call(total, part):
    whole = pl.BlockSpec(memory_space=pltpu.VMEM)
    return pl.pallas_call(
        sum_kernel,
        in_specs=[whole, whole],
        out_specs=whole,
        out_shape=jax.ShapeDtypeStruct(total.shape, total.dtype),
        input_output_aliases={0: 0},
        compiler_params=pltpu.CompilerParams(vmem_limit_bytes=VMEM_LIMIT),
        cost_estimate=pl.CostEstimate(flops=SUM_FLOPS, bytes_accessed=10 * total.size, transcendentals=0),
        name="kv_sum",
    )(total, part)


def last_kernel(total_ref, part_ref, key_ref, value_ref):
    for index, out_ref in enumerate((key_ref, value_ref)):
        whole = total_ref[index] + part_ref[index].astype(jnp.float32)
        out_ref[...] = jnp.transpose(whole, (1, 0, 2)).astype(out_ref.dtype)


def last_call(total, part):
    _, groups, rows, dim = total.shape
    whole = pl.BlockSpec(memory_space=pltpu.VMEM)
    out = jax.ShapeDtypeStruct((rows, groups, dim), jnp.bfloat16)
    return pl.pallas_call(
        last_kernel,
        in_specs=[whole, whole],
        out_specs=(whole, whole),
        out_shape=(out, out),
        compiler_params=pltpu.CompilerParams(vmem_limit_bytes=VMEM_LIMIT),
        cost_estimate=pl.CostEstimate(
            flops=total.size, bytes_accessed=8 * total.size, transcendentals=0
        ),
        name="kv_rows",
    )(total, part)


def shards(query_states, key_states, value_states, out_grad, log_norm, row_delta, doc_lengths):
    rows, heads, dim = query_states.shape
    group = heads // KV_HEADS
    chunk = lax.axis_index("ctx") * lax.axis_size("head") + lax.axis_index("head")
    first_pos = chunk * rows

    kv = jnp.transpose(jnp.stack([key_states, value_states]), (0, 2, 1, 3))
    behind = {distance: chunk_permute(kv, lambda c, d=distance: c + d) for distance in ORDER}

    by_head = lambda x: jnp.transpose(x, (1, 0, 2)).reshape(KV_HEADS, group * rows, dim)
    queries, grads = by_head(query_states), by_head(out_grad)
    distances = jnp.asarray((0, *ORDER), jnp.int32)
    place = jnp.concatenate([jnp.reshape(first_pos, (1,)), distances * rows])
    starts, norms, deltas = rows_call(place, log_norm, row_delta, doc_lengths)

    rows_of = (starts, norms, deltas, queries, grads)
    query_total = None
    returned = []
    for slot, distance in enumerate(ORDER, 1):
        query_total, kv_part = tile_call(slot, *rows_of, behind[distance], query_total)
        returned.append(chunk_permute(kv_part, lambda c, d=distance: c - d))
    query_total, kv_own = tile_call(0, *rows_of, kv, query_total)
    query_heads = query_call(query_total, rows)
    for part in returned[:-1]:
        kv_own = sum_call(kv_own, part)
    key_grad, value_grad = last_call(kv_own, returned[-1])
    query_grad = jnp.transpose(query_heads.reshape(heads, rows, dim), (1, 0, 2))
    return (query_grad, key_grad, value_grad)


def solution(mesh):
    spec3 = P(("ctx", "head"), None, None)
    spec2 = P(("ctx", "head"), None)
    return jax.shard_map(
        shards,
        mesh=mesh,
        in_specs=(spec3, spec3, spec3, spec3, spec2, spec2, P()),
        out_specs=(spec3, spec3, spec3),
        check_vma=False,
    )
```

```python
import functools
import math

import jax
import jax.numpy as jnp
from jax import lax
from jax.experimental import pallas as pl
from jax.experimental.pallas import tpu as pltpu
from jax.sharding import PartitionSpec as P

KV_HEADS = 4
HEAD_DIM = 128
MOST = 512
LOG2E = 1.4426950408889634
VMEM_LIMIT = 40 * 1024 * 1024
SUM_FLOPS = 700_000_000
ORDER = (3, 4, 2, 1)


def chunk_permute(x, target):
    heads, ctxs = lax.axis_size("head"), lax.axis_size("ctx")
    count = heads * ctxs
    place = lambda c: (c % heads) * ctxs + c // heads
    routes = [(c, target(c)) for c in range(count)]
    pairs = [(place(c), place(to)) for c, to in routes if 0 <= to < count]
    return lax.ppermute(x, ("head", "ctx"), pairs)


def contract(left, right, dims):
    return lax.dot_general(
        left, right, ((dims[:1], dims[1:]), ((), ())), preferred_element_type=jnp.float32
    )


def stack_kernel(key_ref, value_ref, out_ref):
    out_ref[0] = key_ref[...]
    out_ref[1] = value_ref[...]


def stack_call(keys, values):
    whole = pl.BlockSpec(memory_space=pltpu.VMEM)
    return pl.pallas_call(
        stack_kernel,
        in_specs=[whole, whole],
        out_specs=whole,
        out_shape=jax.ShapeDtypeStruct((2, *keys.shape), keys.dtype),
        compiler_params=pltpu.CompilerParams(vmem_limit_bytes=VMEM_LIMIT),
        name="kv_stack",
    )(keys, values)


def rows_kernel(place_ref, norm_ref, delta_ref, length_ref, start_ref, norm_out, delta_out):
    groups, _, cols = norm_out.shape
    heads, rows = norm_ref.shape
    docs = length_ref.shape[1]
    norms = norm_ref[...] * LOG2E
    deltas = delta_ref[...]
    for head in range(heads):
        group, at = divmod(head * rows, cols)
        norm_out[group, :, pl.ds(at, rows)] = norms[head : head + 1]
        delta_out[group, :, pl.ds(at, rows)] = deltas[head : head + 1]
    upto = lax.broadcasted_iota(jnp.int32, (docs, docs), 1) <= lax.broadcasted_iota(
        jnp.int32, (docs, docs), 0
    )
    lengths = length_ref[...].astype(jnp.float32)
    ends = jnp.sum(jnp.where(upto, lengths, 0.0), axis=1, keepdims=True)
    first = place_ref[0]
    positions = (lax.broadcasted_iota(jnp.int32, (docs, rows), 1) + first).astype(jnp.float32)
    starts = jnp.max(jnp.where(ends <= positions, ends, 0.0), axis=0, keepdims=True)
    starts = starts.astype(jnp.int32) - first
    for slot in range(start_ref.shape[0]):
        for at in range(0, cols, rows):
            start_ref[slot, :, pl.ds(at, rows)] = starts + place_ref[1 + slot]


def rows_call(place, log_norm, row_delta, doc_lengths):
    rows, heads = log_norm.shape
    cols = heads * rows // KV_HEADS
    whole = pl.BlockSpec(memory_space=pltpu.VMEM)
    slots = place.shape[0] - 1
    wide = jax.ShapeDtypeStruct((KV_HEADS, 1, cols), jnp.float32)
    return pl.pallas_call(
        rows_kernel,
        in_specs=[pl.BlockSpec(memory_space=pltpu.SMEM), whole, whole, whole],
        out_specs=(whole, whole, whole),
        out_shape=(jax.ShapeDtypeStruct((slots, 1, cols), jnp.int32), wide, wide),
        compiler_params=pltpu.CompilerParams(vmem_limit_bytes=VMEM_LIMIT),
        name="row_terms",
    )(place, log_norm.T, row_delta.T, doc_lengths.reshape(1, -1))


def tile_kernel(
    slot,
    softmax_scale,
    start_ref,
    norm_ref,
    delta_ref,
    query_ref,
    grad_ref,
    kv_ref,
    *rest,
):
    query_in_ref = rest[0] if len(rest) == 3 else None
    query_total_ref, kv_part_ref = rest[-2:]
    groups, cols, _ = query_ref.shape
    rows = kv_ref.shape[2]
    key_pos = lax.broadcasted_iota(jnp.int32, (rows, cols), 0)
    allowed = key_pos >= start_ref[slot]
    if slot == 0:
        query_pos = lax.broadcasted_iota(jnp.int32, (rows, cols), 1) & (rows - 1)
        allowed = allowed & (key_pos <= query_pos)
    for group in range(groups):
        keys = kv_ref[0, group]
        values = kv_ref[1, group]
        query_rows = query_ref[group]
        grad_rows = grad_ref[group]
        scores = contract(keys, query_rows, (1, 1))
        prob_grad = contract(values, grad_rows, (1, 1))
        prob = jnp.exp2(scores * (softmax_scale * LOG2E) - norm_ref[group])
        prob = jnp.where(allowed, prob, 0.0)
        score_grad = (prob * (prob_grad - delta_ref[group])).astype(jnp.bfloat16)
        value_part = contract(prob.astype(jnp.bfloat16), grad_rows, (1, 0))
        key_part = contract(score_grad, query_rows, (1, 0)) * softmax_scale
        query_part = contract(keys, score_grad, (0, 0))
        if query_in_ref is not None:
            query_part += query_in_ref[group]
        query_total_ref[group] = query_part
        kv_part_ref[0, group] = key_part.astype(kv_part_ref.dtype)
        kv_part_ref[1, group] = value_part.astype(kv_part_ref.dtype)


def tile_call(slot, starts, norms, deltas, queries, grads, kv, query_total=None):
    groups, cols, dim = queries.shape
    rows = kv.shape[2]
    args = [starts, norms, deltas, queries, grads, kv]
    aliases = {}
    if query_total is not None:
        aliases = {len(args): 0}
        args.append(query_total)
    whole = pl.BlockSpec(memory_space=pltpu.VMEM)
    return pl.pallas_call(
        functools.partial(tile_kernel, slot, 1.0 / math.sqrt(dim)),
        in_specs=[whole] * len(args),
        out_specs=(whole, whole),
        out_shape=(
            jax.ShapeDtypeStruct((groups, dim, cols), jnp.float32),
            jax.ShapeDtypeStruct(kv.shape, jnp.float32 if slot == 0 else jnp.bfloat16),
        ),
        input_output_aliases=aliases,
        compiler_params=pltpu.CompilerParams(vmem_limit_bytes=VMEM_LIMIT),
        cost_estimate=pl.CostEstimate(
            flops=10 * groups * cols * rows * dim,
            bytes_accessed=6 * groups * cols * dim,
            transcendentals=groups * cols * rows,
        ),
        name=f"tiles_{slot}",
    )(*args)


def query_kernel(softmax_scale, total_ref, out_ref):
    groups, heads, rows, _ = out_ref.shape

    def group_step(group, carry):
        for head in range(heads):
            part = total_ref[group, :, pl.ds(head * rows, rows)]
            out_ref[group, head] = (part.T * softmax_scale).astype(out_ref.dtype)
        return carry

    lax.fori_loop(0, groups, group_step, 0)


def query_call(query_total, rows):
    groups, dim, cols = query_total.shape
    whole = pl.BlockSpec(memory_space=pltpu.VMEM)
    return pl.pallas_call(
        functools.partial(query_kernel, 1.0 / math.sqrt(dim)),
        in_specs=[whole],
        out_specs=whole,
        out_shape=jax.ShapeDtypeStruct((groups, cols // rows, rows, dim), jnp.bfloat16),
        compiler_params=pltpu.CompilerParams(vmem_limit_bytes=VMEM_LIMIT),
        cost_estimate=pl.CostEstimate(
            flops=groups * cols * dim, bytes_accessed=6 * groups * cols * dim, transcendentals=0
        ),
        name="query_rows",
    )(query_total)


def sum_kernel(total_ref, part_ref, out_ref):
    out_ref[...] = total_ref[...] + part_ref[...].astype(jnp.float32)


def sum_call(total, part):
    whole = pl.BlockSpec(memory_space=pltpu.VMEM)
    return pl.pallas_call(
        sum_kernel,
        in_specs=[whole, whole],
        out_specs=whole,
        out_shape=jax.ShapeDtypeStruct(total.shape, total.dtype),
        input_output_aliases={0: 0},
        compiler_params=pltpu.CompilerParams(vmem_limit_bytes=VMEM_LIMIT),
        cost_estimate=pl.CostEstimate(flops=SUM_FLOPS, bytes_accessed=10 * total.size, transcendentals=0),
        name="kv_sum",
    )(total, part)


def last_kernel(total_ref, part_ref, key_ref, value_ref):
    for index, out_ref in enumerate((key_ref, value_ref)):
        whole = total_ref[index] + part_ref[index].astype(jnp.float32)
        out_ref[...] = jnp.transpose(whole, (1, 0, 2)).astype(out_ref.dtype)


def last_call(total, part):
    _, groups, rows, dim = total.shape
    whole = pl.BlockSpec(memory_space=pltpu.VMEM)
    out = jax.ShapeDtypeStruct((rows, groups, dim), jnp.bfloat16)
    return pl.pallas_call(
        last_kernel,
        in_specs=[whole, whole],
        out_specs=(whole, whole),
        out_shape=(out, out),
        compiler_params=pltpu.CompilerParams(vmem_limit_bytes=VMEM_LIMIT),
        cost_estimate=pl.CostEstimate(
            flops=total.size, bytes_accessed=8 * total.size, transcendentals=0
        ),
        name="kv_rows",
    )(total, part)


def shards(query_states, key_states, value_states, out_grad, log_norm, row_delta, doc_lengths):
    rows, heads, dim = query_states.shape
    group = heads // KV_HEADS
    chunk = lax.axis_index("ctx") * lax.axis_size("head") + lax.axis_index("head")
    first_pos = chunk * rows

    kv = stack_call(jnp.transpose(key_states, (1, 0, 2)), jnp.transpose(value_states, (1, 0, 2)))
    behind = {distance: chunk_permute(kv, lambda c, d=distance: c + d) for distance in ORDER}

    by_head = lambda x: jnp.transpose(x, (1, 0, 2)).reshape(KV_HEADS, group * rows, dim)
    queries, grads = by_head(query_states), by_head(out_grad)
    distances = jnp.asarray((0, *ORDER), jnp.int32)
    place = jnp.concatenate([jnp.reshape(first_pos, (1,)), distances * rows])
    starts, norms, deltas = rows_call(place, log_norm, row_delta, doc_lengths)

    rows_of = (starts, norms, deltas, queries, grads)
    query_total = None
    returned = []
    for slot, distance in enumerate(ORDER, 1):
        query_total, kv_part = tile_call(slot, *rows_of, behind[distance], query_total)
        returned.append(chunk_permute(kv_part, lambda c, d=distance: c - d))
    query_total, kv_own = tile_call(0, *rows_of, kv, query_total)
    query_heads = query_call(query_total, rows)
    for part in returned[:-1]:
        kv_own = sum_call(kv_own, part)
    key_grad, value_grad = last_call(kv_own, returned[-1])
    query_grad = jnp.transpose(query_heads.reshape(heads, rows, dim), (1, 0, 2))
    return (query_grad, key_grad, value_grad)


def solution(mesh):
    spec3 = P(("ctx", "head"), None, None)
    spec2 = P(("ctx", "head"), None)
    return jax.shard_map(
        shards,
        mesh=mesh,
        in_specs=(spec3, spec3, spec3, spec3, spec2, spec2, P()),
        out_specs=(spec3, spec3, spec3),
        check_vma=False,
    )
```
